32 devices in a mesh: ctx: 8 (over y, x, core), exp: 4 (over z).
Axes of the slice: x: 2, y: 2, z: 4, core: 2. Of those that a mesh axis runs over, the one named last changes fastest.
Arguments:
- residual: bfloat16 [1024, 4096], P(('ctx', 'exp')), may hold values from -6 to 6
- queries: bfloat16 [1024, 4096], P('ctx', 'exp'), may hold values from -8 to 8
- keys: bfloat16 [1024, 256], P('ctx'), may hold values from -8 to 8
- values: bfloat16 [1024, 256], P('ctx'), may hold values from -6 to 6
- span_pos: int32 [16], replicated, may hold values from 0 to 15, each once
- out_proj: bfloat16 [4096, 4096], P('exp'), may hold values from -0.71875 to 0.71875
- norm_gain: float32 [4096], replicated, may hold values from 0.25 to 1.75
- expert_gate: bfloat16 [16, 4096, 768], P('exp', None, 'ctx'), may hold values from -0.09375 to 0.09375
- expert_up: bfloat16 [16, 4096, 768], P('exp', None, 'ctx'), may hold values from -0.09375 to 0.09375
- expert_ids: int32 [1024, 8], P(('ctx', 'exp')), may hold values from 0 to 15, all different within a row; in each aligned block of 32 rows (0 to 31, 32 to 63, ...) at most 24 rows name the same one
- route_weight: float32 [1024, 8], P(('ctx', 'exp')), may hold values from 0.25 to 2
Outputs:
- mixed: bfloat16 [1024, 4096], P(('ctx', 'exp'))
- routed: bfloat16 [1024, 8, 768], P(('ctx', 'exp'))
The draws below stay inside these ranges and needn't reach their ends.
Inputs may be any that keep to these rules, and one draw needn't show every extreme that they name: `span_pos`: every span number appears once. `expert_ids`: each row names 8 different experts; among the rows of one device (32 rows in a row, aligned) no expert is named more than 24 times, and in some device's rows some expert is named exactly 24 times.
All inputs are finite; a program needn't handle non-finite values.
Results may differ from the reference program's by a relative error of at most 0.035.
Values may be sent and summed in bfloat16 or wider, within the bound.
A program may use at most 192 MiB of HBM per device.

```python
import math
import jax
import jax.numpy as jnp
import numpy as np
from jax import lax

D = 4096
HQ = 32
KVH = 2
HD = 128
FE = 768
EXPERTS = 16
TOPK = 8
SEQ = 1024
CH = 64
SPANS = 16
TOK_DEV = 32
MOST = 24
QPD = 8
N_EXP = 4


def query_key_pair(key):
    key_q, key_k = jax.random.split(key, 2)
    query_arr = jnp.clip(jax.random.normal(key_q, (SEQ, HQ * HD), jnp.float32), -4.0, 4.0)
    key_arr = jnp.clip(jax.random.normal(key_k, (SEQ, KVH * HD), jnp.float32), -4.0, 4.0)
    return (query_arr, key_arr)


def draw_queries(key, part):
    return query_key_pair(jax.random.fold_in(key, 7))[0].astype(jnp.bfloat16)


def draw_keys(key, part):
    return query_key_pair(jax.random.fold_in(key, 7))[1].astype(jnp.bfloat16)


def steps_of(stream_key, dims, cuts, smallest, top_value):
    def one(dim, parts):
        draws = jax.random.uniform(jax.random.fold_in(jax.random.fold_in(stream_key, 6), dim), (parts,), jnp.float32, smallest / len(cuts), top_value / len(cuts))
        return jnp.repeat(jnp.exp(draws), dims[dim] // parts).reshape((-1,) + (1,) * (len(dims) - dim - 1))

    loudness = one(*cuts[0])
    for cut in cuts[1:]:
        loudness = loudness * one(*cut)
    return loudness


def routed_block(stream_key, own, number, rows, amount, top, most, lean):
    sequence = jax.random.permutation(stream_key, amount)
    heavy_load, ordinary = portions_of(amount, rows * top, most, lean, True), portions_of(amount, rows * top, most, lean, False)
    places = jnp.arange(amount)

    def named(tallies, rotation):
        used = int((tallies > 0).sum())
        fixed = max(1, used // 4)
        passed = fixed + (places - fixed + rotation * (used - fixed)) % max(1, amount - fixed)
        return jnp.zeros((amount,), jnp.int32).at[sequence[jnp.where(places < fixed, places, passed)]].set(jnp.asarray(tallies, jnp.int32))

    tallies = jnp.where(number % 4 == 0, named(heavy_load, number // 4), named(ordinary, number - number // 4 - 1))
    mixed = jax.random.permutation(jax.random.fold_in(own, 3), amount)
    source_of, sink = mixed[0:amount // 2 * 2:2], mixed[1:amount // 2 * 2:2]
    room = jnp.minimum(tallies[source_of] - 1, most - tallies[sink]) // 2
    room = jnp.where((source_of == sequence[0]) | (sink == sequence[0]) | (tallies[sink] == 0), 0, jnp.maximum(room, 0))
    passed = jax.random.randint(jax.random.fold_in(own, 4), (amount // 2,), 0, 1 << 20) % (room + 1)
    tallies = tallies.at[source_of].add(-passed).at[sink].add(passed)
    items = jnp.searchsorted(jnp.cumsum(tallies), jnp.arange(rows * top), side="right").astype(jnp.int32)
    listing = items.reshape(top, rows).T
    listing = listing[jax.random.permutation(jax.random.fold_in(own, 1), rows)]
    rotation = jax.random.randint(jax.random.fold_in(own, 2), (rows, 1), 0, top)
    return jnp.take_along_axis(listing, (jnp.arange(top)[None, :] + rotation) % top, axis=1)


def portions_of(amount, total, bound, skew, full):
    portions = [(1 << 20) // math.isqrt(standing ** skew) + 1 for standing in range(1, amount + 1)]
    largest = bound if full else min(bound, max(-(-total // amount), total * portions[0] // sum(portions)))
    least = 1 if total - largest >= amount - 1 else 0
    holding, surplus = [largest] + [least] * (amount - 1), total - largest - least * (amount - 1)
    while surplus > 0:
        candidates = [i for i in range(1, amount) if holding[i] < largest] or [i for i in range(1, amount) if holding[i] < bound]
        whole, budget = sum([portions[i] for i in candidates]), surplus
        for i in candidates:
            addition = min(bound - holding[i], max(1, budget * portions[i] // whole), surplus)
            holding[i] = holding[i] + addition
            surplus = surplus - addition
    return np.array(holding)


def bell_draw(rng, extent, scale, reach, cuts=(), held_as=jnp.bfloat16):
    entries = jax.random.normal(rng, extent, jnp.float32) * scale
    if len(cuts) > 0:
        entries = steps_of(rng, extent, cuts, -0.22, 0.18) * entries
    return jnp.clip(entries, min=-reach, max=reach).astype(held_as)


def setup_inputs(seed: int = 0) -> dict:
    key_list = jax.random.split(jax.random.key(seed), 12)
    residual = bell_draw(key_list[0], (SEQ, D), 1.0, 6.0, ((0, 32),))
    queries = draw_queries(jax.random.fold_in(key_list[11], 71), 0)
    keys = draw_keys(jax.random.fold_in(key_list[11], 71), 0)
    values = bell_draw(key_list[3], (SEQ, KVH * HD), 1.0, 6.0, ((0, 8),))
    span_pos = jax.random.permutation(key_list[4], SPANS).astype(jnp.int32)
    out_proj = bell_draw(key_list[5], (HQ * HD, D), 0.12, 0.71875, ((0, 4),))
    norm_gain = jnp.clip(1.0 + 0.15 * jax.random.normal(key_list[6], (D,), jnp.float32), 0.25, 1.75)
    expert_gate = bell_draw(key_list[7], (EXPERTS, D, FE), D ** -0.5, 0.09375, ((0, 4), (2, 8)))
    expert_up = bell_draw(key_list[8], (EXPERTS, D, FE), D ** -0.5, 0.09375, ((0, 4), (2, 8)))
    expert_ids_keys = jax.random.split(jax.random.fold_in(key_list[9], 1), SEQ // TOK_DEV)
    expert_ids_turns = jax.random.permutation(jax.random.fold_in(key_list[9], 3), SEQ // TOK_DEV)
    expert_ids = jax.vmap(lambda own, number: routed_block(jax.random.fold_in(key_list[9], 2), own, number, TOK_DEV, EXPERTS, TOPK, MOST, 2))(expert_ids_keys, expert_ids_turns).reshape((SEQ, TOPK))
    route_weight = jnp.clip(jnp.exp(math.log(2.0) - 2.0794415 * jax.random.uniform(key_list[10], (SEQ, TOPK), jnp.float32) ** steps_of(key_list[10], (SEQ, TOPK), ((0, 32),), -0.2, 0.2)), 0.25, 2.0)
    return {"residual": residual, "queries": queries, "keys": keys, "values": values, "span_pos": span_pos, "out_proj": out_proj, "norm_gain": norm_gain, "expert_gate": expert_gate, "expert_up": expert_up, "expert_ids": expert_ids, "route_weight": route_weight}


def positions(span_pos):
    rows = jnp.arange(SEQ, dtype=jnp.int32)
    return (span_pos[rows // CH] * CH + rows % CH).astype(jnp.int32)

def reference(residual, queries, keys, values, span_pos, out_proj, norm_gain, expert_gate, expert_up, expert_ids, route_weight):
    seq_pos = positions(span_pos)
    visible = seq_pos[None, :] <= seq_pos[:, None]
    scale = 1.0 / math.sqrt(HD)
    group = HQ // KVH

    def one_head(head):
        kv_head = head // group
        query = lax.dynamic_slice_in_dim(queries, head * HD, HD, 1)
        key_part = lax.dynamic_slice_in_dim(keys, kv_head * HD, HD, 1)
        value_part = lax.dynamic_slice_in_dim(values, kv_head * HD, HD, 1)
        scores = jnp.dot(query, key_part.T, preferred_element_type=jnp.float32) * scale
        scores = jnp.where(visible, scores, -1e+30)
        top = lax.optimization_barrier(jnp.max(scores, axis=1, keepdims=True))
        probs = jnp.where(visible, jnp.exp(scores - top), 0.0)
        total = lax.optimization_barrier(jnp.sum(probs, axis=1, keepdims=True))
        summed = jnp.dot(probs.astype(jnp.bfloat16), value_part, preferred_element_type=jnp.float32)
        return (summed / total).astype(jnp.bfloat16)
    heads = lax.map(one_head, jnp.arange(HQ, dtype=jnp.int32))
    attn = jnp.transpose(heads, (1, 0, 2)).reshape(SEQ, HQ * HD)
    width = QPD * HD
    head_total = jnp.zeros((SEQ, D), jnp.float32)
    for group_index in range(N_EXP):
        cols = slice(group_index * width, (group_index + 1) * width)
        share = jnp.dot(attn[:, cols], out_proj[cols], preferred_element_type=jnp.float32).astype(jnp.bfloat16)
        share = lax.optimization_barrier(share)
        head_total = head_total + share.astype(jnp.float32)
    mixed = (residual.astype(jnp.float32) + head_total).astype(jnp.bfloat16)
    mixed_f = mixed.astype(jnp.float32)
    square = lax.optimization_barrier(jnp.mean(mixed_f * mixed_f, axis=1, keepdims=True))
    normed = (mixed_f * lax.rsqrt(square + 1e-06) * norm_gain[None, :]).astype(jnp.bfloat16)

    def one_expert(accum, expert):
        gate = jnp.dot(normed, expert_gate[expert], preferred_element_type=jnp.float32)
        upper = jnp.dot(normed, expert_up[expert], preferred_element_type=jnp.float32)
        hidden = jax.nn.silu(gate) * upper
        chosen = expert_ids == expert
        term = route_weight[:, :, None] * hidden[:, None, :]
        return (accum + jnp.where(chosen[:, :, None], term, 0.0), None)
    start_acc = jnp.zeros((SEQ, TOPK, FE), jnp.float32)
    accum, _ = lax.scan(one_expert, start_acc, jnp.arange(EXPERTS, dtype=jnp.int32))
    return (mixed, accum.astype(jnp.bfloat16))
```

```python
import math

import jax
import jax.numpy as jnp
from jax import lax
from jax.sharding import PartitionSpec as P

D = 4096
HQ = 32
KVH = 2
HD = 128
FE = 768
EXPERTS = 16
TOPK = 8
CH = 64


def stored_positions(span_pos, first, count):
    rows = first + jnp.arange(count, dtype=jnp.int32)
    span = rows // CH
    table = span[:, None] == jnp.arange(span_pos.shape[0], dtype=jnp.int32)[None, :]
    base = jnp.sum(jnp.where(table, span_pos[None, :], 0), axis=1)
    return base * CH + rows % CH


def shards(
    residual,
    queries,
    keys,
    values,
    span_pos,
    out_proj,
    norm_gain,
    expert_gate,
    expert_up,
    expert_ids,
    route_weight,
):
    tok_rows = queries.shape[0]
    per_device = queries.shape[1] // HD
    group = HQ // KVH
    ctx_index = lax.axis_index("ctx")
    exp_index = lax.axis_index("exp")
    kv_head = exp_index * per_device // group
    own_keys = lax.dynamic_slice_in_dim(keys, kv_head * HD, HD, 1)
    own_values = lax.dynamic_slice_in_dim(values, kv_head * HD, HD, 1)
    query_pos = stored_positions(span_pos, ctx_index * tok_rows, tok_rows)
    query_heads = queries.reshape(tok_rows, per_device, HD)
    scale = 1.0 / math.sqrt(HD)
    start_carry = (
        jnp.full((per_device, tok_rows), -1e30, jnp.float32),
        jnp.zeros((per_device, tok_rows), jnp.float32),
        jnp.zeros((per_device, tok_rows, HD), jnp.float32),
    )
    carry = start_carry
    start = jnp.int32(0)
    key_value = lax.all_gather(
        jnp.concatenate((own_keys, own_values), axis=1), "ctx", axis=0, tiled=True
    )
    key_piece, value_piece = key_value[:, :HD], key_value[:, HD:]
    length = key_piece.shape[0]
    block = min(length, 1024)
    for begin in range(0, length, block):
        stop = min(begin + block, length)
        attend_key_piece = key_piece[begin:stop]
        attend_value_piece = value_piece[begin:stop]
        attend_start = start + begin
        attend_running, attend_total, attend_accum = carry
        key_pos = stored_positions(span_pos, attend_start, attend_key_piece.shape[0])
        scores = (
            jnp.einsum(
                "tqd,nd->qtn", query_heads, attend_key_piece, preferred_element_type=jnp.float32
            )
            * scale
        )
        visible = key_pos[None, None, :] <= query_pos[None, :, None]
        block_top = jnp.max(jnp.where(visible, scores, -1e30), axis=2)
        new_top = jnp.maximum(attend_running, block_top)
        factor = jnp.exp(attend_running - new_top)
        probs = jnp.where(visible, jnp.exp(scores - new_top[:, :, None]), 0.0)
        attend_total = attend_total * factor + jnp.sum(probs, axis=2)
        summed = jnp.einsum(
            "qtn,nd->qtd",
            probs.astype(jnp.bfloat16),
            attend_value_piece,
            preferred_element_type=jnp.float32,
        )
        attend_accum = attend_accum * factor[:, :, None] + summed
        carry = (new_top, attend_total, attend_accum)
    running, total, accum = carry
    attn = (accum / total[:, :, None]).astype(jnp.bfloat16)
    attn = jnp.transpose(attn, (1, 0, 2)).reshape(tok_rows, per_device * HD)
    tok_dev = residual.shape[0]
    head_total = lax.psum_scatter(
        jnp.dot(attn, out_proj, preferred_element_type=jnp.float32).astype(jnp.bfloat16),
        "exp",
        scatter_dimension=0,
        tiled=True,
    ).astype(jnp.float32)
    mixed = (residual.astype(jnp.float32) + head_total).astype(jnp.bfloat16)
    mixed_f = mixed.astype(jnp.float32)
    square = jnp.mean(mixed_f * mixed_f, axis=1, keepdims=True)
    normed = (mixed_f * lax.rsqrt(square + 1e-06) * norm_gain[None, :]).astype(jnp.bfloat16)
    every = lax.all_gather(normed, ("ctx", "exp"), axis=0, tiled=True)
    experts, _, width = expert_gate.shape
    devices = every.shape[0] // tok_dev
    weights = jnp.transpose(jnp.stack((expert_gate, expert_up)), (2, 0, 1, 3))
    units = jnp.dot(
        every, weights.reshape(D, 2 * experts * width), preferred_element_type=jnp.float32
    )
    gate, upper = units[:, : experts * width], units[:, experts * width :]
    hidden = (jax.nn.silu(gate) * upper).astype(jnp.bfloat16)
    returned = lax.all_to_all(
        hidden.reshape(devices, tok_dev, experts * width),
        ("ctx", "exp"),
        split_axis=0,
        concat_axis=0,
        tiled=True,
    )
    n_exp = EXPERTS // experts
    returned = returned.reshape(devices // n_exp, n_exp, tok_dev, experts, width)
    returned = jnp.transpose(returned, (2, 1, 3, 0, 4)).reshape(tok_dev * EXPERTS, FE)
    target = jnp.arange(tok_dev, dtype=jnp.int32)[:, None] * EXPERTS + expert_ids
    picked = jnp.take(returned, target.reshape(-1), axis=0).astype(jnp.float32)
    routed = (picked * route_weight.reshape(-1)[:, None]).astype(jnp.bfloat16)
    return (mixed, routed.reshape(tok_dev, TOPK, FE))


def solution(mesh):
    in_specs = (
        P(("ctx", "exp"), None),
        P("ctx", "exp"),
        P("ctx", None),
        P("ctx", None),
        P(),
        P("exp", None),
        P(),
        P("exp", None, "ctx"),
        P("exp", None, "ctx"),
        P(("ctx", "exp"), None),
        P(("ctx", "exp"), None),
    )
    out_specs = (P(("ctx", "exp"), None), P(("ctx", "exp"), None, None))
    return jax.shard_map(shards, mesh=mesh, in_specs=in_specs, out_specs=out_specs, check_vma=False)
```

```python
import functools
import math

import jax
import jax.numpy as jnp
from jax import lax
from jax.experimental import pallas as pl
from jax.experimental.pallas import tpu as pltpu
from jax.sharding import PartitionSpec as P

D = 4096
HQ = 32
KVH = 2
HD = 128
FE = 768
EXPERTS = 16
TOPK = 8
CH = 64


def stored_positions(span_pos, first, count):
    rows = first + jnp.arange(count, dtype=jnp.int32)
    span = rows // CH
    table = span[:, None] == jnp.arange(span_pos.shape[0], dtype=jnp.int32)[None, :]
    base = jnp.sum(jnp.where(table, span_pos[None, :], 0), axis=1)
    return base * CH + rows % CH


MESH = pl.DeviceIdType.MESH


def ring_place(index):
    upper, lower = index // 2, index % 2
    return upper * 2 + (lower + upper) % 2


def expert_kernel(
    n_pos,
    n_exp,
    part,
    residual,
    gain,
    own_weights,
    mixed,
    ret,
    tokens,
    units,
    hidden,
    sums,
    weights,
    w_sem,
    sum_send,
    sum_recv,
    line_send,
    line_recv,
    ring_send,
    ring_recv,
    back_send,
    back_recv,
):
    ctx, exp = lax.axis_index("ctx"), lax.axis_index("exp")
    pos, parity = ctx // 2, ctx % 2
    ring = ring_place(pos)
    half = n_pos // 2
    slots = n_pos * n_exp
    mine = pos * n_exp + exp
    tok_dev = residual.shape[0]
    width = hidden.shape[3]

    def device(place, index):
        return (2 * place + parity, index)

    def remote(src, dst, send, recv, target):
        return pltpu.make_async_remote_copy(
            src_ref=src,
            dst_ref=dst,
            send_sem=send,
            recv_sem=recv,
            device_id=target,
            device_id_type=MESH,
        )

    partner = (2 * pos + 1 - parity, exp)
    barrier = pltpu.get_barrier_semaphore()

    def greet(slot, carry):
        @pl.when(slot != mine)
        def _():
            pl.semaphore_signal(
                barrier, inc=1, device_id=device(slot // n_exp, slot % n_exp), device_id_type=MESH
            )

        return carry

    lax.fori_loop(0, slots, greet, 0)
    pl.semaphore_signal(barrier, inc=1, device_id=partner, device_id_type=MESH)
    pl.semaphore_wait(barrier, slots)

    def sum_copy(step):
        target = (exp + step) % n_exp
        return remote(
            part.at[target],
            sums.at[step - 1],
            sum_send.at[step - 1],
            sum_recv.at[step - 1],
            device(pos, target),
        )

    for step in range(1, n_exp):
        sum_copy(step).start()
    own_copy = pltpu.make_async_copy(own_weights, weights.at[0], w_sem.at[0])
    own_copy.start()
    pair_copy = remote(own_weights, weights.at[1], w_sem.at[1], w_sem.at[2], partner)
    pair_copy.start()

    total = residual[...].astype(jnp.float32) + part[exp].astype(jnp.float32)
    for step in range(1, n_exp):
        sum_copy(step).wait_recv()
        total = total + sums[step - 1].astype(jnp.float32)
    mixed_own = total.astype(jnp.bfloat16)
    mixed[...] = mixed_own
    mixed_f = mixed_own.astype(jnp.float32)
    square = jnp.mean(mixed_f * mixed_f, axis=1, keepdims=True)
    tokens[mine] = (mixed_f * lax.rsqrt(square + 1e-06) * gain[...]).astype(jnp.bfloat16)

    def line_copy(block, way):
        place = tokens.at[pos * n_exp + block]
        return remote(
            place,
            place,
            line_send.at[(way + 1) // 2, block],
            line_recv.at[block],
            device(pos, exp + way),
        )

    def ring_copy(block, hop, way, arrived):
        back = hop if arrived else hop - 1
        origin = ring_place((ring - way * back + n_pos) % n_pos)
        place = tokens.at[origin * n_exp + block]
        if hop == half:
            columns = D // 2
            place = place.at[:, pl.ds(0 if way > 0 else columns, columns)]
        index = (way + 1) // 2
        return remote(
            place,
            place,
            ring_send.at[index, hop - 1, block],
            ring_recv.at[index, hop - 1, block],
            device(ring_place((ring + way + n_pos) % n_pos), exp),
        )

    def blocks_of(step, action):
        if step == 0:
            action(exp, 0)
            return

        @pl.when(exp >= step)
        def _():
            action(exp - step, 1)

        @pl.when(exp + step < n_exp)
        def _():
            action(exp + step, -1)

    def line_sends(block, way, act):
        for out in (1, -1) if way == 0 else (way,):

            @pl.when((exp + out >= 0) & (exp + out < n_exp))
            def _():
                act(line_copy(block, out))

    def line_step(block, way):
        if way != 0:
            line_copy(block, way).wait_recv()
        line_sends(block, way, lambda copy: copy.start())
        for out in (1, -1):
            ring_copy(block, 1, out, False).start()

    def ring_step(hop):
        def action(block, way):
            for out in (1, -1):
                ring_copy(block, hop, out, True).wait_recv()
                if hop < half:
                    ring_copy(block, hop + 1, out, False).start()

        return action

    tile = min(256, weights.shape[2])
    tiles = weights.shape[2] // tile

    def back_copy(place, index):
        slot = place * n_exp + index
        return remote(
            hidden.at[slot],
            ret.at[mine],
            back_send.at[slot],
            back_recv.at[mine],
            device(place, index),
        )

    def back_local(slot):
        return pltpu.make_async_copy(hidden.at[slot], ret.at[slot], back_recv.at[slot])

    def compute(place):
        rows = tokens[pl.ds(place * n_exp, n_exp)]
        if tok_dev % 16:
            rows = rows.astype(jnp.float32).reshape(n_exp * tok_dev, D).astype(jnp.bfloat16)
        else:
            rows = rows.reshape(n_exp * tok_dev, D)
        for which in range(2):
            for index in range(tiles):
                units[:, index * tile : (index + 1) * tile] = jnp.dot(
                    rows,
                    weights[which, :, index * tile : (index + 1) * tile],
                    preferred_element_type=jnp.float32,
                )
            gate, upper = units[:, :width], units[:, width:]
            result = gate / (1.0 + jnp.exp(-gate)) * upper
            side = parity if which == 0 else 1 - parity
            for index in range(n_exp):
                hidden[place * n_exp + index, side] = result[
                    index * tok_dev : (index + 1) * tok_dev
                ].astype(jnp.bfloat16)
        for index in range(n_exp):
            slot = place * n_exp + index

            @pl.when(slot != mine)
            def _():
                back_copy(place, index).start()

            @pl.when(slot == mine)
            def _():
                back_local(slot).start()

    own_copy.wait()
    for step in range(n_exp + half - 1):
        if step < n_exp:
            blocks_of(step, line_step)
        if step == n_exp - 1:
            pair_copy.wait()
            compute(pos)
        for hop in range(1, half):
            if 0 <= step - hop < n_exp:
                blocks_of(step - hop, ring_step(hop))
    for hop in range(1, half):
        for way in (1, -1):
            compute(ring_place((ring + way * hop + n_pos) % n_pos))
    for step in range(n_exp):
        blocks_of(step, ring_step(half))
    compute(ring_place((ring + half) % n_pos))

    for step in range(1, n_exp):
        sum_copy(step).wait_send()

    def finish(block, way):
        line_sends(block, way, lambda copy: copy.wait_send())
        for hop in range(1, half + 1):
            for out in (1, -1):
                ring_copy(block, hop, out, False).wait_send()

    for step in range(n_exp):
        blocks_of(step, finish)

    def collect(slot, carry):
        @pl.when(slot != mine)
        def _():
            back_copy(slot // n_exp, slot % n_exp).wait_send()
            remote(
                hidden.at[slot],
                ret.at[slot],
                back_send.at[slot],
                back_recv.at[slot],
                device(slot // n_exp, slot % n_exp),
            ).wait_recv()

        @pl.when(slot == mine)
        def _():
            back_local(slot).wait()

        return carry

    lax.fori_loop(0, slots, collect, 0)


def expert_layer(n_ctx, n_exp, part, residual, gain, own_weights):
    n_pos = n_ctx // 2
    slots = n_pos * n_exp
    tok_dev = residual.shape[0]
    columns = own_weights.shape[1]
    width = columns // 2
    half = n_pos // 2
    dma = pltpu.SemaphoreType.DMA
    vmem = pl.BlockSpec(memory_space=pltpu.VMEM)
    return pl.pallas_call(
        functools.partial(expert_kernel, n_pos, n_exp),
        out_shape=(
            jax.ShapeDtypeStruct((tok_dev, D), jnp.bfloat16),
            jax.ShapeDtypeStruct((slots, 2, tok_dev, width), jnp.bfloat16),
        ),
        in_specs=[vmem, vmem, vmem, pl.BlockSpec(memory_space=pl.ANY)],
        out_specs=(vmem, vmem),
        scratch_shapes=[
            pltpu.VMEM((slots, tok_dev, D), jnp.bfloat16),
            pltpu.VMEM((n_exp * tok_dev, columns), jnp.float32),
            pltpu.VMEM((slots, 2, tok_dev, width), jnp.bfloat16),
            pltpu.VMEM((n_exp - 1, tok_dev, D), jnp.bfloat16),
            pltpu.VMEM((2, D, columns), jnp.bfloat16),
            dma((3,)),
            dma((n_exp - 1,)),
            dma((n_exp - 1,)),
            dma((2, n_exp)),
            dma((n_exp,)),
            dma((2, half, n_exp)),
            dma((2, half, n_exp)),
            dma((slots,)),
            dma((slots,)),
        ],
        compiler_params=pltpu.CompilerParams(
            collective_id=0, has_side_effects=True, vmem_limit_bytes=48 * 1024 * 1024
        ),
        cost_estimate=pl.CostEstimate(
            flops=4 * slots * tok_dev * D * columns, bytes_accessed=1 << 23, transcendentals=0
        ),
    )(part, residual, gain, own_weights)


def shards(
    n_ctx,
    n_exp,
    residual,
    queries,
    keys,
    values,
    span_pos,
    out_proj,
    norm_gain,
    expert_gate,
    expert_up,
    expert_ids,
    route_weight,
):
    tok_rows = queries.shape[0]
    per_device = queries.shape[1] // HD
    group = HQ // KVH
    ctx_index = lax.axis_index("ctx")
    exp_index = lax.axis_index("exp")
    kv_head = exp_index * per_device // group
    own_keys = lax.dynamic_slice_in_dim(keys, kv_head * HD, HD, 1)
    own_values = lax.dynamic_slice_in_dim(values, kv_head * HD, HD, 1)
    query_pos = stored_positions(span_pos, ctx_index * tok_rows, tok_rows)
    query_heads = queries.reshape(tok_rows, per_device, HD)
    scale = 1.0 / math.sqrt(HD)
    start_carry = (
        jnp.full((per_device, tok_rows), -1e30, jnp.float32),
        jnp.zeros((per_device, tok_rows), jnp.float32),
        jnp.zeros((per_device, tok_rows, HD), jnp.float32),
    )
    carry = start_carry
    start = jnp.int32(0)
    key_value = lax.all_gather(
        jnp.concatenate((own_keys, own_values), axis=1), "ctx", axis=0, tiled=True
    )
    key_piece, value_piece = key_value[:, :HD], key_value[:, HD:]
    length = key_piece.shape[0]
    block = min(length, 1024)
    for begin in range(0, length, block):
        stop = min(begin + block, length)
        attend_key_piece = key_piece[begin:stop]
        attend_value_piece = value_piece[begin:stop]
        attend_start = start + begin
        attend_running, attend_total, attend_accum = carry
        key_pos = stored_positions(span_pos, attend_start, attend_key_piece.shape[0])
        scores = (
            jnp.einsum(
                "tqd,nd->qtn", query_heads, attend_key_piece, preferred_element_type=jnp.float32
            )
            * scale
        )
        visible = key_pos[None, None, :] <= query_pos[None, :, None]
        block_top = jnp.max(jnp.where(visible, scores, -1e30), axis=2)
        new_top = jnp.maximum(attend_running, block_top)
        factor = jnp.exp(attend_running - new_top)
        probs = jnp.where(visible, jnp.exp(scores - new_top[:, :, None]), 0.0)
        attend_total = attend_total * factor + jnp.sum(probs, axis=2)
        summed = jnp.einsum(
            "qtn,nd->qtd",
            probs.astype(jnp.bfloat16),
            attend_value_piece,
            preferred_element_type=jnp.float32,
        )
        attend_accum = attend_accum * factor[:, :, None] + summed
        carry = (new_top, attend_total, attend_accum)
    running, total, accum = carry
    attn = (accum / total[:, :, None]).astype(jnp.bfloat16)
    attn = jnp.transpose(attn, (1, 0, 2)).reshape(tok_rows, per_device * HD)
    tok_dev = residual.shape[0]
    part = jnp.dot(attn, out_proj, preferred_element_type=jnp.float32).astype(jnp.bfloat16)
    experts, _, width = expert_gate.shape
    own_weights = jnp.transpose(jnp.stack((expert_gate, expert_up)), (2, 0, 1, 3))
    mixed, returned = expert_layer(
        n_ctx,
        n_exp,
        part.reshape(n_exp, tok_dev, D),
        residual,
        norm_gain[None, :],
        own_weights.reshape(D, 2 * experts * width),
    )
    returned = returned.reshape(n_ctx // 2, n_exp, 2, tok_dev, experts, width)
    returned = jnp.transpose(returned, (3, 1, 4, 0, 2, 5)).reshape(tok_dev * EXPERTS, FE)
    target = jnp.arange(tok_dev, dtype=jnp.int32)[:, None] * EXPERTS + expert_ids
    picked = jnp.take(returned, target.reshape(-1), axis=0).astype(jnp.float32)
    routed = (picked * route_weight.reshape(-1)[:, None]).astype(jnp.bfloat16)
    return (mixed, routed.reshape(tok_dev, TOPK, FE))


def solution(mesh):
    in_specs = (
        P(("ctx", "exp"), None),
        P("ctx", "exp"),
        P("ctx", None),
        P("ctx", None),
        P(),
        P("exp", None),
        P(),
        P("exp", None, "ctx"),
        P("exp", None, "ctx"),
        P(("ctx", "exp"), None),
        P(("ctx", "exp"), None),
    )
    out_specs = (P(("ctx", "exp"), None), P(("ctx", "exp"), None, None))
    body = functools.partial(shards, mesh.shape["ctx"], mesh.shape["exp"])
    return jax.shard_map(body, mesh=mesh, in_specs=in_specs, out_specs=out_specs, check_vma=False)
```

```python
import functools
import math

import jax
import jax.numpy as jnp
from jax import lax
from jax.experimental import pallas as pl
from jax.experimental.pallas import tpu as pltpu
from jax.sharding import PartitionSpec as P

D = 4096
HQ = 32
KVH = 2
HD = 128
FE = 768
EXPERTS = 16
TOPK = 8
CH = 64


def stored_positions(span_pos, first, count):
    rows = first + jnp.arange(count, dtype=jnp.int32)
    span = rows // CH
    table = span[:, None] == jnp.arange(span_pos.shape[0], dtype=jnp.int32)[None, :]
    base = jnp.sum(jnp.where(table, span_pos[None, :], 0), axis=1)
    return base * CH + rows % CH


CHUNKS = 2
MESH = pl.DeviceIdType.MESH


def ring_place(index):
    upper, lower = index // 2, index % 2
    return upper * 2 + (lower + upper) % 2


def expert_kernel(
    n_pos,
    n_exp,
    part,
    residual,
    gain,
    own_gate,
    own_upper,
    mixed,
    ret,
    tokens,
    normed,
    units,
    hidden,
    sums,
    weights,
    w_sem,
    sum_send,
    sum_recv,
    line_send,
    line_recv,
    ring_send,
    ring_recv,
    back_send,
    back_recv,
):
    ctx, exp = lax.axis_index("ctx"), lax.axis_index("exp")
    pos, parity = ctx // 2, ctx % 2
    ring = ring_place(pos)
    half = n_pos // 2
    slots = n_pos * n_exp
    mine = pos * n_exp + exp
    tok_dev = residual.shape[0]
    width = hidden.shape[3]
    padded = weights.shape[1] // 2
    chunk = D // CHUNKS

    def device(place, index):
        return (2 * place + parity, index)

    def remote(src, dst, send, recv, target):
        return pltpu.make_async_remote_copy(
            src_ref=src,
            dst_ref=dst,
            send_sem=send,
            recv_sem=recv,
            device_id=target,
            device_id_type=MESH,
        )

    partner = (2 * pos + 1 - parity, exp)
    barrier = pltpu.get_barrier_semaphore()

    def greet(slot, carry):
        @pl.when(slot != mine)
        def _():
            pl.semaphore_signal(
                barrier, inc=1, device_id=device(slot // n_exp, slot % n_exp), device_id_type=MESH
            )

        return carry

    lax.fori_loop(0, slots, greet, 0)
    pl.semaphore_signal(barrier, inc=1, device_id=partner, device_id_type=MESH)
    pl.semaphore_wait(barrier, slots)

    def columns_of(piece):
        return pl.ds(piece * chunk, chunk)

    def sum_copy(step, piece):
        target = (exp + step) % n_exp
        return remote(
            part.at[target, :, columns_of(piece)],
            sums.at[step - 1, :, columns_of(piece)],
            sum_send.at[step - 1, piece],
            sum_recv.at[step - 1, piece],
            device(pos, target),
        )

    def own_copy(which):
        return pltpu.make_async_copy(
            (own_gate, own_upper)[which],
            weights.at[0, pl.ds(which * padded, width)],
            w_sem.at[0, which],
        )

    def pair_copy(which):
        return remote(
            (own_gate, own_upper)[which],
            weights.at[1, pl.ds(which * padded, width)],
            w_sem.at[1, which],
            w_sem.at[2, which],
            partner,
        )

    for piece in range(CHUNKS):
        for step in range(1, n_exp):
            sum_copy(step, piece).start()
    for which in range(2):
        own_copy(which).start()
        pair_copy(which).start()

    def add_up(piece):
        columns = slice(piece * chunk, (piece + 1) * chunk)
        total = residual[:, columns].astype(jnp.float32)
        total = total + part[exp, :, columns].astype(jnp.float32)
        for step in range(1, n_exp):
            sum_copy(step, piece).wait_recv()
            total = total + sums[step - 1, :, columns].astype(jnp.float32)
        total = total.astype(jnp.bfloat16)
        mixed[:, columns] = total
        tokens[mine, :, columns] = total

    def line_copy(block, way, piece):
        place = tokens.at[pos * n_exp + block, :, columns_of(piece)]
        return remote(
            place,
            place,
            line_send.at[(way + 1) // 2, block, piece],
            line_recv.at[block, piece],
            device(pos, exp + way),
        )

    def ring_copy(block, hop, way, arrived, piece):
        back = hop if arrived else hop - 1
        origin = ring_place((ring - way * back + n_pos) % n_pos)
        first, columns = piece * chunk, chunk
        if hop == half:
            columns = chunk // 2
            first += 0 if way > 0 else columns
        place = tokens.at[origin * n_exp + block, :, pl.ds(first, columns)]
        index = (way + 1) // 2
        return remote(
            place,
            place,
            ring_send.at[index, hop - 1, block, piece],
            ring_recv.at[index, hop - 1, block, piece],
            device(ring_place((ring + way + n_pos) % n_pos), exp),
        )

    def blocks_of(step, action):
        if step == 0:
            action(exp, 0)
            return

        @pl.when(exp >= step)
        def _():
            action(exp - step, 1)

        @pl.when(exp + step < n_exp)
        def _():
            action(exp + step, -1)

    def line_sends(block, way, piece, act):
        for out in (1, -1) if way == 0 else (way,):

            @pl.when((exp + out >= 0) & (exp + out < n_exp))
            def _():
                act(line_copy(block, out, piece))

    def line_step(piece):
        def action(block, way):
            if way != 0:
                line_copy(block, way, piece).wait_recv()
            line_sends(block, way, piece, lambda copy: copy.start())
            for out in (1, -1):
                ring_copy(block, 1, out, False, piece).start()

        return action

    def ring_step(hop, piece):
        def action(block, way):
            for out in (1, -1):
                ring_copy(block, hop, out, True, piece).wait_recv()
                if hop < half:
                    ring_copy(block, hop + 1, out, False, piece).start()

        return action

    tile = min(256, 2 * padded)
    tiles = 2 * padded // tile

    def back_copy(place, index):
        slot = place * n_exp + index
        return remote(
            hidden.at[slot],
            ret.at[mine],
            back_send.at[slot],
            back_recv.at[mine],
            device(place, index),
        )

    def back_local(slot):
        return pltpu.make_async_copy(hidden.at[slot], ret.at[slot], back_recv.at[slot])

    def compute(place):
        for index in range(n_exp):
            row = tokens[place * n_exp + index].astype(jnp.float32)
            square = jnp.mean(row * row, axis=1, keepdims=True)
            normed[index] = (row * lax.rsqrt(square + 1e-06) * gain[...]).astype(jnp.bfloat16)
        rows = normed[...]
        if tok_dev % 16:
            rows = rows.astype(jnp.float32).reshape(n_exp * tok_dev, D).astype(jnp.bfloat16)
        else:
            rows = rows.reshape(n_exp * tok_dev, D)
        for which in range(2):
            for index in range(tiles):
                units[:, index * tile : (index + 1) * tile] = lax.dot_general(
                    rows,
                    weights[which, index * tile : (index + 1) * tile],
                    (((1,), (1,)), ((), ())),
                    preferred_element_type=jnp.float32,
                )
            gate, upper = units[:, :width], units[:, padded : padded + width]
            result = gate / (1.0 + jnp.exp(-gate)) * upper
            side = parity if which == 0 else 1 - parity
            for index in range(n_exp):
                hidden[place * n_exp + index, side] = result[
                    index * tok_dev : (index + 1) * tok_dev
                ].astype(jnp.bfloat16)
        for index in range(n_exp):
            slot = place * n_exp + index

            @pl.when(slot != mine)
            def _():
                back_copy(place, index).start()

            @pl.when(slot == mine)
            def _():
                back_local(slot).start()

    lag = 2
    for time in range(n_exp + half - 1 + lag * (CHUNKS - 1)):
        for piece in reversed(range(CHUNKS)):
            step = time - lag * piece
            if step == 0:
                add_up(piece)
            if 0 <= step < n_exp:
                blocks_of(step, line_step(piece))
            if step == n_exp - 1 and piece == CHUNKS - 1:
                for which in range(2):
                    own_copy(which).wait()
                    pair_copy(which).wait()
                compute(pos)
        for piece in range(CHUNKS):
            for hop in range(1, half):
                step = time - lag * piece - hop
                if 0 <= step < n_exp:
                    blocks_of(step, ring_step(hop, piece))
    for hop in range(1, half):
        for way in (1, -1):
            compute(ring_place((ring + way * hop + n_pos) % n_pos))
    for piece in range(CHUNKS):
        for step in range(n_exp):
            blocks_of(step, ring_step(half, piece))
    compute(ring_place((ring + half) % n_pos))

    for piece in range(CHUNKS):
        for step in range(1, n_exp):
            sum_copy(step, piece).wait_send()

        def finish(block, way):
            line_sends(block, way, piece, lambda copy: copy.wait_send())
            for hop in range(1, half + 1):
                for out in (1, -1):
                    ring_copy(block, hop, out, False, piece).wait_send()

        for step in range(n_exp):
            blocks_of(step, finish)

    def collect(slot, carry):
        @pl.when(slot != mine)
        def _():
            back_copy(slot // n_exp, slot % n_exp).wait_send()
            remote(
                hidden.at[slot],
                ret.at[slot],
                back_send.at[slot],
                back_recv.at[slot],
                device(slot // n_exp, slot % n_exp),
            ).wait_recv()

        @pl.when(slot == mine)
        def _():
            back_local(slot).wait()

        return carry

    lax.fori_loop(0, slots, collect, 0)


def expert_layer(n_ctx, n_exp, part, residual, gain, own_gate, own_upper):
    n_pos = n_ctx // 2
    slots = n_pos * n_exp
    tok_dev = residual.shape[0]
    width = own_gate.shape[0]
    padded = -(-width // 16) * 16
    half = n_pos // 2
    dma = pltpu.SemaphoreType.DMA
    vmem = pl.BlockSpec(memory_space=pltpu.VMEM)
    return pl.pallas_call(
        functools.partial(expert_kernel, n_pos, n_exp),
        out_shape=(
            jax.ShapeDtypeStruct((tok_dev, D), jnp.bfloat16),
            jax.ShapeDtypeStruct((slots, 2, tok_dev, width), jnp.bfloat16),
        ),
        in_specs=[vmem, vmem, vmem] + [pl.BlockSpec(memory_space=pl.ANY)] * 2,
        out_specs=(vmem, vmem),
        scratch_shapes=[
            pltpu.VMEM((slots, tok_dev, D), jnp.bfloat16),
            pltpu.VMEM((n_exp, tok_dev, D), jnp.bfloat16),
            pltpu.VMEM((n_exp * tok_dev, 2 * padded), jnp.float32),
            pltpu.VMEM((slots, 2, tok_dev, width), jnp.bfloat16),
            pltpu.VMEM((n_exp - 1, tok_dev, D), jnp.bfloat16),
            pltpu.VMEM((2, 2 * padded, D), jnp.bfloat16),
            dma((3, 2)),
            dma((n_exp - 1, CHUNKS)),
            dma((n_exp - 1, CHUNKS)),
            dma((2, n_exp, CHUNKS)),
            dma((n_exp, CHUNKS)),
            dma((2, half, n_exp, CHUNKS)),
            dma((2, half, n_exp, CHUNKS)),
            dma((slots,)),
            dma((slots,)),
        ],
        compiler_params=pltpu.CompilerParams(
            collective_id=0, has_side_effects=True, vmem_limit_bytes=48 * 1024 * 1024
        ),
        cost_estimate=pl.CostEstimate(
            flops=8 * slots * tok_dev * D * width, bytes_accessed=1 << 23, transcendentals=0
        ),
    )(part, residual, gain, own_gate, own_upper)


def shards(
    n_ctx,
    n_exp,
    residual,
    queries,
    keys,
    values,
    span_pos,
    out_proj,
    norm_gain,
    expert_gate,
    expert_up,
    expert_ids,
    route_weight,
):
    tok_rows = queries.shape[0]
    per_device = queries.shape[1] // HD
    group = HQ // KVH
    ctx_index = lax.axis_index("ctx")
    exp_index = lax.axis_index("exp")
    kv_head = exp_index * per_device // group
    own_keys = lax.dynamic_slice_in_dim(keys, kv_head * HD, HD, 1)
    own_values = lax.dynamic_slice_in_dim(values, kv_head * HD, HD, 1)
    query_pos = stored_positions(span_pos, ctx_index * tok_rows, tok_rows)
    query_heads = queries.reshape(tok_rows, per_device, HD)
    scale = 1.0 / math.sqrt(HD)
    start_carry = (
        jnp.full((per_device, tok_rows), -1e30, jnp.float32),
        jnp.zeros((per_device, tok_rows), jnp.float32),
        jnp.zeros((per_device, tok_rows, HD), jnp.float32),
    )
    carry = start_carry
    start = jnp.int32(0)
    key_value = lax.all_gather(
        jnp.concatenate((own_keys, own_values), axis=1), "ctx", axis=0, tiled=True
    )
    key_piece, value_piece = key_value[:, :HD], key_value[:, HD:]
    length = key_piece.shape[0]
    block = min(length, 1024)
    for begin in range(0, length, block):
        stop = min(begin + block, length)
        attend_key_piece = key_piece[begin:stop]
        attend_value_piece = value_piece[begin:stop]
        attend_start = start + begin
        attend_running, attend_total, attend_accum = carry
        key_pos = stored_positions(span_pos, attend_start, attend_key_piece.shape[0])
        scores = (
            jnp.einsum(
                "tqd,nd->qtn", query_heads, attend_key_piece, preferred_element_type=jnp.float32
            )
            * scale
        )
        visible = key_pos[None, None, :] <= query_pos[None, :, None]
        block_top = jnp.max(jnp.where(visible, scores, -1e30), axis=2)
        new_top = jnp.maximum(attend_running, block_top)
        factor = jnp.exp(attend_running - new_top)
        probs = jnp.where(visible, jnp.exp(scores - new_top[:, :, None]), 0.0)
        attend_total = attend_total * factor + jnp.sum(probs, axis=2)
        summed = jnp.einsum(
            "qtn,nd->qtd",
            probs.astype(jnp.bfloat16),
            attend_value_piece,
            preferred_element_type=jnp.float32,
        )
        attend_accum = attend_accum * factor[:, :, None] + summed
        carry = (new_top, attend_total, attend_accum)
    running, total, accum = carry
    attn = (accum / total[:, :, None]).astype(jnp.bfloat16)
    attn = jnp.transpose(attn, (1, 0, 2)).reshape(tok_rows, per_device * HD)
    tok_dev = residual.shape[0]
    part = jnp.dot(attn, out_proj, preferred_element_type=jnp.float32).astype(jnp.bfloat16)
    experts, _, width = expert_gate.shape
    mixed, returned = expert_layer(
        n_ctx,
        n_exp,
        part.reshape(n_exp, tok_dev, D),
        residual,
        norm_gain[None, :],
        jnp.transpose(expert_gate, (0, 2, 1)).reshape(experts * width, D),
        jnp.transpose(expert_up, (0, 2, 1)).reshape(experts * width, D),
    )
    returned = returned.reshape(n_ctx // 2, n_exp, 2, tok_dev, experts, width)
    returned = jnp.transpose(returned, (3, 1, 4, 0, 2, 5)).reshape(tok_dev * EXPERTS, FE)
    target = jnp.arange(tok_dev, dtype=jnp.int32)[:, None] * EXPERTS + expert_ids
    picked = jnp.take(returned, target.reshape(-1), axis=0).astype(jnp.float32)
    routed = (picked * route_weight.reshape(-1)[:, None]).astype(jnp.bfloat16)
    return (mixed, routed.reshape(tok_dev, TOPK, FE))


def solution(mesh):
    in_specs = (
        P(("ctx", "exp"), None),
        P("ctx", "exp"),
        P("ctx", None),
        P("ctx", None),
        P(),
        P("exp", None),
        P(),
        P("exp", None, "ctx"),
        P("exp", None, "ctx"),
        P(("ctx", "exp"), None),
        P(("ctx", "exp"), None),
    )
    out_specs = (P(("ctx", "exp"), None), P(("ctx", "exp"), None, None))
    body = functools.partial(shards, mesh.shape["ctx"], mesh.shape["exp"])
    return jax.shard_map(body, mesh=mesh, in_specs=in_specs, out_specs=out_specs, check_vma=False)
```

```python
import functools
import math

import jax
import jax.numpy as jnp
from jax import lax
from jax.experimental import pallas as pl
from jax.experimental.pallas import tpu as pltpu
from jax.sharding import PartitionSpec as P

D = 4096
HQ = 32
KVH = 2
HD = 128
FE = 768
EXPERTS = 16
TOPK = 8
CH = 64


def stored_positions(span_pos, first, count):
    rows = first + jnp.arange(count, dtype=jnp.int32)
    span = rows // CH
    table = span[:, None] == jnp.arange(span_pos.shape[0], dtype=jnp.int32)[None, :]
    base = jnp.sum(jnp.where(table, span_pos[None, :], 0), axis=1)
    return base * CH + rows % CH


CHUNKS = 2
MESH = pl.DeviceIdType.MESH


def ring_place(index):
    upper, lower = index // 2, index % 2
    return upper * 2 + (lower + upper) % 2


def expert_kernel(
    n_pos,
    n_exp,
    part,
    residual,
    gain,
    own_gate,
    own_upper,
    mixed,
    ret,
    tokens,
    normed,
    flipped,
    units,
    hidden,
    sums,
    weights,
    w_sem,
    sum_send,
    sum_recv,
    line_send,
    line_recv,
    ring_send,
    ring_recv,
    back_send,
    back_recv,
):
    ctx, exp = lax.axis_index("ctx"), lax.axis_index("exp")
    pos, parity = ctx // 2, ctx % 2
    ring = ring_place(pos)
    half = n_pos // 2
    slots = n_pos * n_exp
    mine = pos * n_exp + exp
    tok_dev = residual.shape[0]
    width = hidden.shape[3]
    padded = weights.shape[1] // 2
    chunk = D // CHUNKS

    def device(place, index):
        return (2 * place + parity, index)

    def remote(src, dst, send, recv, target):
        return pltpu.make_async_remote_copy(
            src_ref=src,
            dst_ref=dst,
            send_sem=send,
            recv_sem=recv,
            device_id=target,
            device_id_type=MESH,
        )

    partner = (2 * pos + 1 - parity, exp)
    barrier = pltpu.get_barrier_semaphore()

    def greet(slot, carry):
        @pl.when(slot != mine)
        def _():
            pl.semaphore_signal(
                barrier, inc=1, device_id=device(slot // n_exp, slot % n_exp), device_id_type=MESH
            )

        return carry

    lax.fori_loop(0, slots, greet, 0)
    pl.semaphore_signal(barrier, inc=1, device_id=partner, device_id_type=MESH)
    pl.semaphore_wait(barrier, slots)

    def columns_of(piece):
        return pl.ds(piece * chunk, chunk)

    def sum_copy(step, piece):
        target = (exp + step) % n_exp
        return remote(
            part.at[target, :, columns_of(piece)],
            sums.at[step - 1, :, columns_of(piece)],
            sum_send.at[step - 1, piece],
            sum_recv.at[step - 1, piece],
            device(pos, target),
        )

    def own_copy(which):
        return pltpu.make_async_copy(
            (own_gate, own_upper)[which],
            weights.at[0, pl.ds(which * padded, width)],
            w_sem.at[0, which],
        )

    def pair_copy(which):
        return remote(
            (own_gate, own_upper)[which],
            weights.at[1, pl.ds(which * padded, width)],
            w_sem.at[1, which],
            w_sem.at[2, which],
            partner,
        )

    for piece in range(CHUNKS):
        for step in range(1, n_exp):
            sum_copy(step, piece).start()
    for which in range(2):
        own_copy(which).start()
        pair_copy(which).start()

    def add_up(piece):
        columns = slice(piece * chunk, (piece + 1) * chunk)
        total = residual[:, columns].astype(jnp.float32)
        total = total + part[exp, :, columns].astype(jnp.float32)
        for step in range(1, n_exp):
            sum_copy(step, piece).wait_recv()
            total = total + sums[step - 1, :, columns].astype(jnp.float32)
        total = total.astype(jnp.bfloat16)
        mixed[:, columns] = total
        tokens[mine, :, columns] = total

    def line_copy(block, way, piece):
        place = tokens.at[pos * n_exp + block, :, columns_of(piece)]
        return remote(
            place,
            place,
            line_send.at[(way + 1) // 2, block, piece],
            line_recv.at[block, piece],
            device(pos, exp + way),
        )

    def ring_copy(block, hop, way, arrived, piece):
        back = hop if arrived else hop - 1
        origin = ring_place((ring - way * back + n_pos) % n_pos)
        first, columns = piece * chunk, chunk
        if hop == half:
            columns = chunk // 2
            first += 0 if way > 0 else columns
        place = tokens.at[origin * n_exp + block, :, pl.ds(first, columns)]
        index = (way + 1) // 2
        return remote(
            place,
            place,
            ring_send.at[index, hop - 1, block, piece],
            ring_recv.at[index, hop - 1, block, piece],
            device(ring_place((ring + way + n_pos) % n_pos), exp),
        )

    def blocks_of(step, action):
        if step == 0:
            action(exp, 0)
            return

        @pl.when(exp >= step)
        def _():
            action(exp - step, 1)

        @pl.when(exp + step < n_exp)
        def _():
            action(exp + step, -1)

    def line_sends(block, way, piece, act):
        for out in (1, -1) if way == 0 else (way,):

            @pl.when((exp + out >= 0) & (exp + out < n_exp))
            def _():
                act(line_copy(block, out, piece))

    def line_step(piece):
        def action(block, way):
            if way != 0:
                line_copy(block, way, piece).wait_recv()
            line_sends(block, way, piece, lambda copy: copy.start())
            for out in (1, -1):
                ring_copy(block, 1, out, False, piece).start()

        return action

    def ring_step(hop, piece):
        def action(block, way):
            for out in (1, -1):
                ring_copy(block, hop, out, True, piece).wait_recv()
                if hop < half:
                    ring_copy(block, hop + 1, out, False, piece).start()

        return action

    many = n_exp * tok_dev
    slab = math.gcd(D, 512)

    def back_copy(place, index):
        slot = place * n_exp + index
        return remote(
            hidden.at[slot],
            ret.at[mine],
            back_send.at[slot],
            back_recv.at[mine],
            device(place, index),
        )

    def back_local(slot):
        return pltpu.make_async_copy(hidden.at[slot], ret.at[slot], back_recv.at[slot])

    def prepare(places):
        for number, place in enumerate(places):
            for index in range(n_exp):
                row = tokens[place * n_exp + index].astype(jnp.float32)
                square = jnp.mean(row * row, axis=1, keepdims=True)
                row = row * lax.rsqrt(square + 1e-06) * gain[...]
                if tok_dev % 16 == 0:
                    row = row.astype(jnp.bfloat16)
                normed[pl.ds(index * tok_dev, tok_dev)] = row.astype(normed.dtype)
            for first in range(0, D, slab):
                flipped[first : first + slab, number * many : (number + 1) * many] = (
                    normed[:, first : first + slab].astype(jnp.bfloat16).T
                )

    def expand(places, which):
        amount = len(places) * many
        for first in (0, padded):
            units[first : first + padded, :amount] = jnp.dot(
                weights[which, first : first + padded],
                flipped[:, :amount],
                preferred_element_type=jnp.float32,
            )
        gate, upper = units[:padded, :amount], units[padded:, :amount]
        result = (gate / (1.0 + jnp.exp(-gate)) * upper).T
        side = parity if which == 0 else 1 - parity
        for number, place in enumerate(places):
            for index in range(n_exp):
                first = number * many + index * tok_dev
                hidden[place * n_exp + index, side] = result[
                    first : first + tok_dev, :width
                ].astype(jnp.bfloat16)

    def give_back(place):
        for index in range(n_exp):
            slot = place * n_exp + index

            @pl.when(slot != mine)
            def _():
                back_copy(place, index).start()

            @pl.when(slot == mine)
            def _():
                back_local(slot).start()

    def compute(places):
        prepare(places)
        for which in range(2):
            expand(places, which)
        for place in places:
            give_back(place)

    lag = 2
    for time in range(n_exp + half - 1 + lag * (CHUNKS - 1)):
        for piece in reversed(range(CHUNKS)):
            step = time - lag * piece
            if step == 0:
                add_up(piece)
            if 0 <= step < n_exp:
                blocks_of(step, line_step(piece))
            if step == n_exp - 1 and piece == CHUNKS - 1:
                for which in range(2):
                    own_copy(which).wait()
                    pair_copy(which).wait()
                prepare((pos,))
                expand((pos,), 0)
            if step == n_exp and piece == CHUNKS - 1:
                expand((pos,), 1)
                give_back(pos)
        for piece in range(CHUNKS):
            for hop in range(1, half):
                step = time - lag * piece - hop
                if 0 <= step < n_exp:
                    blocks_of(step, ring_step(hop, piece))
    for hop in range(1, half):
        compute([ring_place((ring + way * hop + n_pos) % n_pos) for way in (1, -1)])
    for piece in range(CHUNKS):
        for step in range(n_exp):
            blocks_of(step, ring_step(half, piece))
    compute((ring_place((ring + half) % n_pos),))

    for piece in range(CHUNKS):
        for step in range(1, n_exp):
            sum_copy(step, piece).wait_send()

        def finish(block, way):
            line_sends(block, way, piece, lambda copy: copy.wait_send())
            for hop in range(1, half + 1):
                for out in (1, -1):
                    ring_copy(block, hop, out, False, piece).wait_send()

        for step in range(n_exp):
            blocks_of(step, finish)

    def collect(slot, carry):
        @pl.when(slot != mine)
        def _():
            back_copy(slot // n_exp, slot % n_exp).wait_send()
            remote(
                hidden.at[slot],
                ret.at[slot],
                back_send.at[slot],
                back_recv.at[slot],
                device(slot // n_exp, slot % n_exp),
            ).wait_recv()

        @pl.when(slot == mine)
        def _():
            back_local(slot).wait()

        return carry

    lax.fori_loop(0, slots, collect, 0)


def expert_layer(n_ctx, n_exp, part, residual, gain, own_gate, own_upper):
    n_pos = n_ctx // 2
    slots = n_pos * n_exp
    tok_dev = residual.shape[0]
    width = own_gate.shape[0]
    padded = -(-width // 128) * 128
    many = n_exp * tok_dev
    held = jnp.float32 if tok_dev % 16 else jnp.bfloat16
    half = n_pos // 2
    dma = pltpu.SemaphoreType.DMA
    vmem = pl.BlockSpec(memory_space=pltpu.VMEM)
    return pl.pallas_call(
        functools.partial(expert_kernel, n_pos, n_exp),
        out_shape=(
            jax.ShapeDtypeStruct((tok_dev, D), jnp.bfloat16),
            jax.ShapeDtypeStruct((slots, 2, tok_dev, width), jnp.bfloat16),
        ),
        in_specs=[vmem, vmem, vmem] + [pl.BlockSpec(memory_space=pl.ANY)] * 2,
        out_specs=(vmem, vmem),
        scratch_shapes=[
            pltpu.VMEM((slots, tok_dev, D), jnp.bfloat16),
            pltpu.VMEM((many, D), held),
            pltpu.VMEM((D, 2 * many), jnp.bfloat16),
            pltpu.VMEM((2 * padded, 2 * many), jnp.float32),
            pltpu.VMEM((slots, 2, tok_dev, width), jnp.bfloat16),
            pltpu.VMEM((n_exp - 1, tok_dev, D), jnp.bfloat16),
            pltpu.VMEM((2, 2 * padded, D), jnp.bfloat16),
            dma((3, 2)),
            dma((n_exp - 1, CHUNKS)),
            dma((n_exp - 1, CHUNKS)),
            dma((2, n_exp, CHUNKS)),
            dma((n_exp, CHUNKS)),
            dma((2, half, n_exp, CHUNKS)),
            dma((2, half, n_exp, CHUNKS)),
            dma((slots,)),
            dma((slots,)),
        ],
        compiler_params=pltpu.CompilerParams(
            collective_id=0, has_side_effects=True, vmem_limit_bytes=48 * 1024 * 1024
        ),
        cost_estimate=pl.CostEstimate(
            flops=8 * slots * tok_dev * D * width, bytes_accessed=1 << 23, transcendentals=0
        ),
    )(part, residual, gain, own_gate, own_upper)


def shards(
    n_ctx,
    n_exp,
    residual,
    queries,
    keys,
    values,
    span_pos,
    out_proj,
    norm_gain,
    expert_gate,
    expert_up,
    expert_ids,
    route_weight,
):
    tok_rows = queries.shape[0]
    per_device = queries.shape[1] // HD
    group = HQ // KVH
    ctx_index = lax.axis_index("ctx")
    exp_index = lax.axis_index("exp")
    kv_head = exp_index * per_device // group
    own_keys = lax.dynamic_slice_in_dim(keys, kv_head * HD, HD, 1)
    own_values = lax.dynamic_slice_in_dim(values, kv_head * HD, HD, 1)
    query_pos = stored_positions(span_pos, ctx_index * tok_rows, tok_rows)
    query_heads = queries.reshape(tok_rows, per_device, HD)
    scale = 1.0 / math.sqrt(HD)
    start_carry = (
        jnp.full((per_device, tok_rows), -1e30, jnp.float32),
        jnp.zeros((per_device, tok_rows), jnp.float32),
        jnp.zeros((per_device, tok_rows, HD), jnp.float32),
    )
    carry = start_carry
    start = jnp.int32(0)
    key_value = lax.all_gather(
        jnp.concatenate((own_keys, own_values), axis=1), "ctx", axis=0, tiled=True
    )
    key_piece, value_piece = key_value[:, :HD], key_value[:, HD:]
    length = key_piece.shape[0]
    block = min(length, 1024)
    for begin in range(0, length, block):
        stop = min(begin + block, length)
        attend_key_piece = key_piece[begin:stop]
        attend_value_piece = value_piece[begin:stop]
        attend_start = start + begin
        attend_running, attend_total, attend_accum = carry
        key_pos = stored_positions(span_pos, attend_start, attend_key_piece.shape[0])
        scores = (
            jnp.einsum(
                "tqd,nd->qtn", query_heads, attend_key_piece, preferred_element_type=jnp.float32
            )
            * scale
        )
        visible = key_pos[None, None, :] <= query_pos[None, :, None]
        block_top = jnp.max(jnp.where(visible, scores, -1e30), axis=2)
        new_top = jnp.maximum(attend_running, block_top)
        factor = jnp.exp(attend_running - new_top)
        probs = jnp.where(visible, jnp.exp(scores - new_top[:, :, None]), 0.0)
        attend_total = attend_total * factor + jnp.sum(probs, axis=2)
        summed = jnp.einsum(
            "qtn,nd->qtd",
            probs.astype(jnp.bfloat16),
            attend_value_piece,
            preferred_element_type=jnp.float32,
        )
        attend_accum = attend_accum * factor[:, :, None] + summed
        carry = (new_top, attend_total, attend_accum)
    running, total, accum = carry
    attn = (accum / total[:, :, None]).astype(jnp.bfloat16)
    attn = jnp.transpose(attn, (1, 0, 2)).reshape(tok_rows, per_device * HD)
    tok_dev = residual.shape[0]
    part = jnp.dot(attn, out_proj, preferred_element_type=jnp.float32).astype(jnp.bfloat16)
    experts, _, width = expert_gate.shape
    mixed, returned = expert_layer(
        n_ctx,
        n_exp,
        part.reshape(n_exp, tok_dev, D),
        residual,
        norm_gain[None, :],
        jnp.transpose(expert_gate, (0, 2, 1)).reshape(experts * width, D),
        jnp.transpose(expert_up, (0, 2, 1)).reshape(experts * width, D),
    )
    returned = returned.reshape(n_ctx // 2, n_exp, 2, tok_dev, experts, width)
    returned = jnp.transpose(returned, (3, 1, 4, 0, 2, 5)).reshape(tok_dev * EXPERTS, FE)
    target = jnp.arange(tok_dev, dtype=jnp.int32)[:, None] * EXPERTS + expert_ids
    picked = jnp.take(returned, target.reshape(-1), axis=0).astype(jnp.float32)
    routed = (picked * route_weight.reshape(-1)[:, None]).astype(jnp.bfloat16)
    return (mixed, routed.reshape(tok_dev, TOPK, FE))


def solution(mesh):
    in_specs = (
        P(("ctx", "exp"), None),
        P("ctx", "exp"),
        P("ctx", None),
        P("ctx", None),
        P(),
        P("exp", None),
        P(),
        P("exp", None, "ctx"),
        P("exp", None, "ctx"),
        P(("ctx", "exp"), None),
        P(("ctx", "exp"), None),
    )
    out_specs = (P(("ctx", "exp"), None), P(("ctx", "exp"), None, None))
    body = functools.partial(shards, mesh.shape["ctx"], mesh.shape["exp"])
    return jax.shard_map(body, mesh=mesh, in_specs=in_specs, out_specs=out_specs, check_vma=False)
```

```python
import functools
import math

import jax
import jax.numpy as jnp
from jax import lax
from jax.experimental import pallas as pl
from jax.experimental.pallas import tpu as pltpu
from jax.sharding import PartitionSpec as P

D = 4096
HQ = 32
KVH = 2
HD = 128
FE = 768
EXPERTS = 16
TOPK = 8
CH = 64


def stored_positions(span_pos, first, count):
    rows = first + jnp.arange(count, dtype=jnp.int32)
    span = rows // CH
    table = span[:, None] == jnp.arange(span_pos.shape[0], dtype=jnp.int32)[None, :]
    base = jnp.sum(jnp.where(table, span_pos[None, :], 0), axis=1)
    return base * CH + rows % CH


CHUNKS = 1
MESH = pl.DeviceIdType.MESH


def ring_place(index):
    upper, lower = index // 2, index % 2
    return upper * 2 + (lower + upper) % 2


def expert_kernel(
    n_pos,
    n_exp,
    part,
    residual,
    gain,
    own_gate,
    own_upper,
    mixed,
    ret,
    tokens,
    normed,
    flipped,
    units,
    hidden,
    sums,
    weights,
    w_sem,
    sum_send,
    sum_recv,
    line_send,
    line_recv,
    ring_send,
    ring_recv,
    back_send,
    back_recv,
):
    ctx, exp = lax.axis_index("ctx"), lax.axis_index("exp")
    pos, parity = ctx // 2, ctx % 2
    ring = ring_place(pos)
    half = n_pos // 2
    slots = n_pos * n_exp
    mine = pos * n_exp + exp
    tok_dev = residual.shape[0]
    width = hidden.shape[3]
    padded = weights.shape[1] // 2
    chunk = D // CHUNKS

    def device(place, index):
        return (2 * place + parity, index)

    def remote(src, dst, send, recv, target):
        return pltpu.make_async_remote_copy(
            src_ref=src,
            dst_ref=dst,
            send_sem=send,
            recv_sem=recv,
            device_id=target,
            device_id_type=MESH,
        )

    partner = (2 * pos + 1 - parity, exp)
    barrier = pltpu.get_barrier_semaphore()

    def greet(slot, carry):
        @pl.when(slot != mine)
        def _():
            pl.semaphore_signal(
                barrier, inc=1, device_id=device(slot // n_exp, slot % n_exp), device_id_type=MESH
            )

        return carry

    lax.fori_loop(0, slots, greet, 0)
    pl.semaphore_signal(barrier, inc=1, device_id=partner, device_id_type=MESH)
    pl.semaphore_wait(barrier, slots)

    def columns_of(piece):
        return pl.ds(piece * chunk, chunk)

    def sum_copy(step, piece):
        target = (exp + step) % n_exp
        return remote(
            part.at[target, :, columns_of(piece)],
            sums.at[step - 1, :, columns_of(piece)],
            sum_send.at[step - 1, piece],
            sum_recv.at[step - 1, piece],
            device(pos, target),
        )

    def own_copy(which):
        return pltpu.make_async_copy(
            (own_gate, own_upper)[which],
            weights.at[0, pl.ds(which * padded, width)],
            w_sem.at[0, which],
        )

    def pair_copy(which):
        return remote(
            (own_gate, own_upper)[which],
            weights.at[1, pl.ds(which * padded, width)],
            w_sem.at[1, which],
            w_sem.at[2, which],
            partner,
        )

    for piece in range(CHUNKS):
        for step in range(1, n_exp):
            sum_copy(step, piece).start()
    for which in range(2):
        own_copy(which).start()
        pair_copy(which).start()

    def add_up(piece):
        columns = slice(piece * chunk, (piece + 1) * chunk)
        total = residual[:, columns].astype(jnp.float32)
        total = total + part[exp, :, columns].astype(jnp.float32)
        for step in range(1, n_exp):
            sum_copy(step, piece).wait_recv()
            total = total + sums[step - 1, :, columns].astype(jnp.float32)
        total = total.astype(jnp.bfloat16)
        mixed[:, columns] = total
        tokens[mine, :, columns] = total

    def line_copy(block, way, piece):
        place = tokens.at[pos * n_exp + block, :, columns_of(piece)]
        return remote(
            place,
            place,
            line_send.at[(way + 1) // 2, block, piece],
            line_recv.at[block, piece],
            device(pos, exp + way),
        )

    def ring_copy(block, hop, way, arrived, piece):
        back = hop if arrived else hop - 1
        origin = ring_place((ring - way * back + n_pos) % n_pos)
        first, columns = piece * chunk, chunk
        if hop == half:
            columns = chunk // 2
            first += 0 if way > 0 else columns
        place = tokens.at[origin * n_exp + block, :, pl.ds(first, columns)]
        index = (way + 1) // 2
        return remote(
            place,
            place,
            ring_send.at[index, hop - 1, block, piece],
            ring_recv.at[index, hop - 1, block, piece],
            device(ring_place((ring + way + n_pos) % n_pos), exp),
        )

    def blocks_of(step, action):
        if step == 0:
            action(exp, 0)
            return

        @pl.when(exp >= step)
        def _():
            action(exp - step, 1)

        @pl.when(exp + step < n_exp)
        def _():
            action(exp + step, -1)

    def line_sends(block, way, piece, act):
        for out in (1, -1) if way == 0 else (way,):

            @pl.when((exp + out >= 0) & (exp + out < n_exp))
            def _():
                act(line_copy(block, out, piece))

    def line_step(piece):
        def action(block, way):
            if way != 0:
                line_copy(block, way, piece).wait_recv()
            line_sends(block, way, piece, lambda copy: copy.start())
            for out in (1, -1):
                ring_copy(block, 1, out, False, piece).start()

        return action

    def ring_step(hop, piece):
        def action(block, way):
            for out in (1, -1):
                ring_copy(block, hop, out, True, piece).wait_recv()
                if hop < half:
                    ring_copy(block, hop + 1, out, False, piece).start()

        return action

    many = n_exp * tok_dev
    slab = math.gcd(D, 512)

    def back_copy(place, index):
        slot = place * n_exp + index
        return remote(
            hidden.at[slot],
            ret.at[mine],
            back_send.at[slot],
            back_recv.at[mine],
            device(place, index),
        )

    def back_local(slot):
        return pltpu.make_async_copy(hidden.at[slot], ret.at[slot], back_recv.at[slot])

    def prepare(places):
        for number, place in enumerate(places):
            for index in range(n_exp):
                row = tokens[place * n_exp + index].astype(jnp.float32)
                square = jnp.mean(row * row, axis=1, keepdims=True)
                row = row * lax.rsqrt(square + 1e-06) * gain[...]
                if tok_dev % 16 == 0:
                    row = row.astype(jnp.bfloat16)
                normed[pl.ds(index * tok_dev, tok_dev)] = row.astype(normed.dtype)
            for first in range(0, D, slab):
                flipped[first : first + slab, number * many : (number + 1) * many] = (
                    normed[:, first : first + slab].astype(jnp.bfloat16).T
                )

    def expand(places, which):
        amount = len(places) * many
        for first in (0, padded):
            units[first : first + padded, :amount] = jnp.dot(
                weights[which, first : first + padded],
                flipped[:, :amount],
                preferred_element_type=jnp.float32,
            )
        gate, upper = units[:padded, :amount], units[padded:, :amount]
        result = (gate / (1.0 + jnp.exp(-gate)) * upper).T
        side = parity if which == 0 else 1 - parity
        for number, place in enumerate(places):
            for index in range(n_exp):
                first = number * many + index * tok_dev
                hidden[place * n_exp + index, side] = result[
                    first : first + tok_dev, :width
                ].astype(jnp.bfloat16)

    def give_back(place):
        for index in range(n_exp):
            slot = place * n_exp + index

            @pl.when(slot != mine)
            def _():
                back_copy(place, index).start()

            @pl.when(slot == mine)
            def _():
                back_local(slot).start()

    def compute(places):
        prepare(places)
        for which in range(2):
            expand(places, which)
        for place in places:
            give_back(place)

    lag = 2
    for time in range(n_exp + half - 1 + lag * (CHUNKS - 1)):
        for piece in reversed(range(CHUNKS)):
            step = time - lag * piece
            if step == 0:
                add_up(piece)
            if 0 <= step < n_exp:
                blocks_of(step, line_step(piece))
            if step == n_exp - 1 and piece == CHUNKS - 1:
                for which in range(2):
                    own_copy(which).wait()
                    pair_copy(which).wait()
                prepare((pos,))
                expand((pos,), 0)
            if step == n_exp and piece == CHUNKS - 1:
                expand((pos,), 1)
                give_back(pos)
        for piece in range(CHUNKS):
            for hop in range(1, half):
                step = time - lag * piece - hop
                if 0 <= step < n_exp:
                    blocks_of(step, ring_step(hop, piece))
    for hop in range(1, half):
        compute([ring_place((ring + way * hop + n_pos) % n_pos) for way in (1, -1)])
    for piece in range(CHUNKS):
        for step in range(n_exp):
            blocks_of(step, ring_step(half, piece))
    compute((ring_place((ring + half) % n_pos),))

    for piece in range(CHUNKS):
        for step in range(1, n_exp):
            sum_copy(step, piece).wait_send()

        def finish(block, way):
            line_sends(block, way, piece, lambda copy: copy.wait_send())
            for hop in range(1, half + 1):
                for out in (1, -1):
                    ring_copy(block, hop, out, False, piece).wait_send()

        for step in range(n_exp):
            blocks_of(step, finish)

    def collect(slot, carry):
        @pl.when(slot != mine)
        def _():
            back_copy(slot // n_exp, slot % n_exp).wait_send()
            remote(
                hidden.at[slot],
                ret.at[slot],
                back_send.at[slot],
                back_recv.at[slot],
                device(slot // n_exp, slot % n_exp),
            ).wait_recv()

        @pl.when(slot == mine)
        def _():
            back_local(slot).wait()

        return carry

    lax.fori_loop(0, slots, collect, 0)


def expert_layer(n_ctx, n_exp, part, residual, gain, own_gate, own_upper):
    n_pos = n_ctx // 2
    slots = n_pos * n_exp
    tok_dev = residual.shape[0]
    width = own_gate.shape[0]
    padded = -(-width // 128) * 128
    many = n_exp * tok_dev
    held = jnp.float32 if tok_dev % 16 else jnp.bfloat16
    half = n_pos // 2
    dma = pltpu.SemaphoreType.DMA
    vmem = pl.BlockSpec(memory_space=pltpu.VMEM)
    return pl.pallas_call(
        functools.partial(expert_kernel, n_pos, n_exp),
        out_shape=(
            jax.ShapeDtypeStruct((tok_dev, D), jnp.bfloat16),
            jax.ShapeDtypeStruct((slots, 2, tok_dev, width), jnp.bfloat16),
        ),
        in_specs=[vmem, vmem, vmem] + [pl.BlockSpec(memory_space=pl.ANY)] * 2,
        out_specs=(vmem, vmem),
        scratch_shapes=[
            pltpu.VMEM((slots, tok_dev, D), jnp.bfloat16),
            pltpu.VMEM((many, D), held),
            pltpu.VMEM((D, 2 * many), jnp.bfloat16),
            pltpu.VMEM((2 * padded, 2 * many), jnp.float32),
            pltpu.VMEM((slots, 2, tok_dev, width), jnp.bfloat16),
            pltpu.VMEM((n_exp - 1, tok_dev, D), jnp.bfloat16),
            pltpu.VMEM((2, 2 * padded, D), jnp.bfloat16),
            dma((3, 2)),
            dma((n_exp - 1, CHUNKS)),
            dma((n_exp - 1, CHUNKS)),
            dma((2, n_exp, CHUNKS)),
            dma((n_exp, CHUNKS)),
            dma((2, half, n_exp, CHUNKS)),
            dma((2, half, n_exp, CHUNKS)),
            dma((slots,)),
            dma((slots,)),
        ],
        compiler_params=pltpu.CompilerParams(
            collective_id=0, has_side_effects=True, vmem_limit_bytes=48 * 1024 * 1024
        ),
        cost_estimate=pl.CostEstimate(
            flops=8 * slots * tok_dev * D * width, bytes_accessed=1 << 23, transcendentals=0
        ),
    )(part, residual, gain, own_gate, own_upper)


def shards(
    n_ctx,
    n_exp,
    residual,
    queries,
    keys,
    values,
    span_pos,
    out_proj,
    norm_gain,
    expert_gate,
    expert_up,
    expert_ids,
    route_weight,
):
    tok_rows = queries.shape[0]
    per_device = queries.shape[1] // HD
    group = HQ // KVH
    ctx_index = lax.axis_index("ctx")
    exp_index = lax.axis_index("exp")
    kv_head = exp_index * per_device // group
    own_keys = lax.dynamic_slice_in_dim(keys, kv_head * HD, HD, 1)
    own_values = lax.dynamic_slice_in_dim(values, kv_head * HD, HD, 1)
    query_pos = stored_positions(span_pos, ctx_index * tok_rows, tok_rows)
    query_heads = queries.reshape(tok_rows, per_device, HD)
    scale = 1.0 / math.sqrt(HD)
    start_carry = (
        jnp.full((per_device, tok_rows), -1e30, jnp.float32),
        jnp.zeros((per_device, tok_rows), jnp.float32),
        jnp.zeros((per_device, tok_rows, HD), jnp.float32),
    )
    carry = start_carry
    start = jnp.int32(0)
    key_value = lax.all_gather(
        jnp.concatenate((own_keys, own_values), axis=1), "ctx", axis=0, tiled=True
    )
    key_piece, value_piece = key_value[:, :HD], key_value[:, HD:]
    length = key_piece.shape[0]
    block = min(length, 1024)
    for begin in range(0, length, block):
        stop = min(begin + block, length)
        attend_key_piece = key_piece[begin:stop]
        attend_value_piece = value_piece[begin:stop]
        attend_start = start + begin
        attend_running, attend_total, attend_accum = carry
        key_pos = stored_positions(span_pos, attend_start, attend_key_piece.shape[0])
        scores = (
            jnp.einsum(
                "tqd,nd->qtn", query_heads, attend_key_piece, preferred_element_type=jnp.float32
            )
            * scale
        )
        visible = key_pos[None, None, :] <= query_pos[None, :, None]
        block_top = jnp.max(jnp.where(visible, scores, -1e30), axis=2)
        new_top = jnp.maximum(attend_running, block_top)
        factor = jnp.exp(attend_running - new_top)
        probs = jnp.where(visible, jnp.exp(scores - new_top[:, :, None]), 0.0)
        attend_total = attend_total * factor + jnp.sum(probs, axis=2)
        summed = jnp.einsum(
            "qtn,nd->qtd",
            probs.astype(jnp.bfloat16),
            attend_value_piece,
            preferred_element_type=jnp.float32,
        )
        attend_accum = attend_accum * factor[:, :, None] + summed
        carry = (new_top, attend_total, attend_accum)
    running, total, accum = carry
    attn = (accum / total[:, :, None]).astype(jnp.bfloat16)
    attn = jnp.transpose(attn, (1, 0, 2)).reshape(tok_rows, per_device * HD)
    tok_dev = residual.shape[0]
    part = jnp.dot(attn, out_proj, preferred_element_type=jnp.float32).astype(jnp.bfloat16)
    experts, _, width = expert_gate.shape
    mixed, returned = expert_layer(
        n_ctx,
        n_exp,
        part.reshape(n_exp, tok_dev, D),
        residual,
        norm_gain[None, :],
        jnp.transpose(expert_gate, (0, 2, 1)).reshape(experts * width, D),
        jnp.transpose(expert_up, (0, 2, 1)).reshape(experts * width, D),
    )
    returned = returned.reshape(n_ctx // 2, n_exp, 2, tok_dev, experts, width)
    returned = jnp.transpose(returned, (3, 1, 4, 0, 2, 5)).reshape(tok_dev * EXPERTS, FE)
    target = jnp.arange(tok_dev, dtype=jnp.int32)[:, None] * EXPERTS + expert_ids
    picked = jnp.take(returned, target.reshape(-1), axis=0).astype(jnp.float32)
    routed = (picked * route_weight.reshape(-1)[:, None]).astype(jnp.bfloat16)
    return (mixed, routed.reshape(tok_dev, TOPK, FE))


def solution(mesh):
    in_specs = (
        P(("ctx", "exp"), None),
        P("ctx", "exp"),
        P("ctx", None),
        P("ctx", None),
        P(),
        P("exp", None),
        P(),
        P("exp", None, "ctx"),
        P("exp", None, "ctx"),
        P(("ctx", "exp"), None),
        P(("ctx", "exp"), None),
    )
    out_specs = (P(("ctx", "exp"), None), P(("ctx", "exp"), None, None))
    body = functools.partial(shards, mesh.shape["ctx"], mesh.shape["exp"])
    return jax.shard_map(body, mesh=mesh, in_specs=in_specs, out_specs=out_specs, check_vma=False)
```
